32 devices in a mesh: groups: 2 (over x), loop: 16 (over z, y, core).
Axes of the slice: x: 2, y: 2, z: 4, core: 2. Of those that a mesh axis runs over, the one named last changes fastest.
Arguments:
- queries: bfloat16 [16384, 2560], P(('groups', 'loop')), parts along dimension 0, may hold values from -6 to 6
- cur_keys: bfloat16 [16384, 2560], P(('groups', 'loop')), parts along dimension 0, may hold values from -6 to 6
- cur_values: bfloat16 [16384, 2560], P(('groups', 'loop')), parts along dimension 0, may hold values from -6 to 6
- past_keys: bfloat16 [1536, 16, 2560], P(('groups', 'loop')), parts along dimension 0, may hold values from -6 to 6
- past_values: bfloat16 [1536, 16, 2560], P(('groups', 'loop')), parts along dimension 0, may hold values from -6 to 6
- pattern: int32 [128, 8], P(('groups', 'loop')), parts along dimension 0, may hold values 0 or 1
- read_blocks: int32 [128, 8], P('groups'), parts along dimension 0, may hold values from 0 to 767, as said below
- out_weight: bfloat16 [2560, 5120], P('loop'), may hold values from -2 to 2
Outputs:
- projected: bfloat16 [16384, 5120], P(('groups', 'loop')), parts along dimension 0
The draws below stay inside these ranges and needn't reach their ends.
There are 2 independent parts, one for each index of `groups`. The reference program is written for one: setup_inputs(seed, part) draws one part's arguments, and reference() takes and returns one part's arrays. A program takes and returns all parts, laid end to end along the dimension named above; an argument that names none is the same for every part. Nothing has to cross between parts.
Inputs may be any that keep to these rules, and one draw needn't show every extreme that they name: `read_blocks`: entries are block numbers of past_keys; block g belongs to region g // 48. In every region the lists of its 4 query blocks together name blocks of each region exactly 2 times.
All inputs are finite; a program needn't handle non-finite values. No bound on the sum of `pattern` on one device may be relied on, other than what follows from the above.
Results may differ from the reference program's by a relative error of at most 0.0057.
Values may be sent and summed in bfloat16 or wider, within the bound.
A program may use at most 192 MiB of HBM per device.

```python
import jax
import jax.numpy as jnp
from jax import lax

D = 5120
HEADS = 20
HD = 128
TOK_DEV = 512
QBLK = 128
KB = 16
R = 8
KT = 48
HW = 2560
NQB = 4
TOKENS = 8192
QBALL = 64
PICKS = 2
N_LOOP = 16


def draw_queries(key, part):
    normal_draw = jax.random.truncated_normal(jax.random.fold_in(key, 1), -6.0, 6.0, (TOKENS, HW), jnp.float32)
    return normal_draw.astype(jnp.bfloat16)


def draw_cur_keys(key, part):
    normal_draw = jax.random.truncated_normal(jax.random.fold_in(key, 2), -6.0, 6.0, (TOKENS, HW), jnp.float32)
    return normal_draw.astype(jnp.bfloat16)


def draw_read_blocks(key, part):
    list_count = NQB * R
    reader_keys = jax.random.split(jax.random.fold_in(key, 21), N_LOOP)
    shuffled = jax.vmap(lambda one_key: jax.random.permutation(one_key, list_count))(reader_keys)
    owners = shuffled // PICKS
    slots = jax.random.randint(jax.random.fold_in(key, 22), (N_LOOP, list_count), 0, KT)
    reader = jnp.arange(N_LOOP)[:, None]
    slots = jnp.where((reader == 0) & (owners == N_LOOP - 1), KT - 1, slots)
    slots = jnp.where((reader == 0) & (owners == 0), 0, slots)
    return (owners * KT + slots).reshape(QBALL, R).astype(jnp.int32)


def touch_ends(values, key, smallest, top_value):
    place = [jax.random.randint(jax.random.fold_in(key, axis), (), 0, length) for axis, length in enumerate(values.shape)]
    widest = values.shape.index(max(values.shape))
    beside = place[:widest] + [(place[widest] + 1) % values.shape[widest]] + place[widest + 1:]
    return values.at[tuple(place)].set(smallest).at[tuple(beside)].set(top_value)


def steps_of(rng, dims, shards, low, top_value):
    factor_of, own = 1.0, jax.random.fold_in(rng, 6)
    for dim, blocks in shards:
        draws = jnp.exp(jax.random.uniform(jax.random.fold_in(own, dim), (blocks,), jnp.float32, low / len(shards), top_value / len(shards)))
        factor_of = factor_of * jnp.repeat(draws, dims[dim] // blocks).reshape([-1 if axis == dim else 1 for axis in range(len(dims))])
    return factor_of


def scatter_about(key, dims, width, limit, pieces=(), kind=jnp.bfloat16):
    values = jax.random.normal(key, dims, jnp.float32) * width
    if len(pieces) > 0:
        values = steps_of(key, dims, pieces, -0.22, 0.18) * values
    return jnp.clip(values, min=-limit, max=limit).astype(kind)


def setup_inputs(seed: int = 0, part: int = 0) -> dict:
    key_of = jax.random.split(jax.random.key(seed), 9)
    part_splits = jax.random.split(jax.random.fold_in(key_of[8], part), 9)
    return {
        "queries": draw_queries(jax.random.fold_in(jax.random.fold_in(key_of[8], part), 71), part),
        "cur_keys": draw_cur_keys(jax.random.fold_in(jax.random.fold_in(key_of[8], part), 71), part),
        "cur_values": scatter_about(part_splits[2], (TOKENS, HW), 1.0, 6.0, ((0, 16),)),
        "past_keys": scatter_about(part_splits[3], (N_LOOP * KT, KB, HW), 1.0, 6.0, ((0, 16),)),
        "past_values": scatter_about(part_splits[4], (N_LOOP * KT, KB, HW), 1.0, 6.0, ((0, 16),)),
        "pattern": touch_ends((jax.random.randint(part_splits[5], (QBALL, 2 * NQB), 0, 2) < 1).astype(jnp.int32), jax.random.fold_in(part_splits[5], 1), 0, 1),
        "read_blocks": draw_read_blocks(jax.random.fold_in(jax.random.fold_in(key_of[8], part), 71), part),
        "out_weight": scatter_about(key_of[7], (HW, D), (max(HW // 256, 1)) ** -0.5, 2.0, ((0, 16),)),
    }


NEG = -1e30


def to_float(values):
    return values.astype(jnp.float32)


def to_half(values):
    return lax.optimization_barrier(values.astype(jnp.bfloat16)).astype(jnp.float32)


def attend(q_part, k_sess, v_sess, allowed, k_local, v_local, k_remote, v_remote, score_scale):
    score_sess = jnp.einsum('bqhd,khd->bhqk', to_float(q_part), to_float(k_sess)) * score_scale
    score_sess = jnp.where(allowed[:, None, None, :], score_sess, NEG)
    score_local = jnp.einsum('bqhd,khd->bhqk', to_float(q_part), to_float(k_local)) * score_scale
    score_remote = jnp.einsum('bqhd,bkhd->bhqk', to_float(q_part), to_float(k_remote)) * score_scale
    row_max = jnp.maximum(jnp.maximum(score_sess.max(-1), score_local.max(-1)), score_remote.max(-1))[..., None]
    weight_sess = jnp.exp(score_sess - row_max)
    weight_local = jnp.exp(score_local - row_max)
    weight_remote = jnp.exp(score_remote - row_max)
    row_total = weight_sess.sum(-1) + weight_local.sum(-1) + weight_remote.sum(-1)
    mixed_sum = jnp.einsum('bhqk,khd->bqhd', to_half(weight_sess), to_float(v_sess))
    mixed_sum = mixed_sum + jnp.einsum('bhqk,khd->bqhd', to_half(weight_local), to_float(v_local))
    mixed_sum = mixed_sum + jnp.einsum('bhqk,bkhd->bqhd', to_half(weight_remote), to_float(v_remote))
    result = mixed_sum / jnp.transpose(row_total, (0, 2, 1))[..., None]
    return result.astype(jnp.bfloat16)


def reference(queries, cur_keys, cur_values, past_keys, past_values, pattern, read_blocks, out_weight):
    score_scale = HD ** -0.5

    def one_device(device):
        q_part = lax.dynamic_slice_in_dim(queries, device * TOK_DEV, TOK_DEV, 0).reshape(NQB, QBLK, HEADS, HD)
        pair_start = (device // 2) * (2 * TOK_DEV)
        k_sess = lax.dynamic_slice_in_dim(cur_keys, pair_start, 2 * TOK_DEV, 0).reshape(2 * TOK_DEV, HEADS, HD)
        v_sess = lax.dynamic_slice_in_dim(cur_values, pair_start, 2 * TOK_DEV, 0).reshape(2 * TOK_DEV, HEADS, HD)
        k_local = lax.dynamic_slice_in_dim(past_keys, device * KT, KT, 0).reshape(KT * KB, HEADS, HD)
        v_local = lax.dynamic_slice_in_dim(past_values, device * KT, KT, 0).reshape(KT * KB, HEADS, HD)
        block_ids = lax.dynamic_slice_in_dim(read_blocks, device * NQB, NQB, 0)
        k_remote = jnp.take(past_keys, block_ids, axis=0).reshape(NQB, R * KB, HEADS, HD)
        v_remote = jnp.take(past_values, block_ids, axis=0).reshape(NQB, R * KB, HEADS, HD)
        pat_rows = lax.dynamic_slice_in_dim(pattern, device * NQB, NQB, 0)
        own_block = (device % 2) * NQB + jnp.arange(NQB, dtype=jnp.int32)
        block_ok = (pat_rows > 0) | (jnp.arange(2 * NQB, dtype=jnp.int32)[None, :] == own_block[:, None])
        allowed = jnp.repeat(block_ok, QBLK, axis=1)
        result = attend(q_part, k_sess, v_sess, allowed, k_local, v_local, k_remote, v_remote, score_scale)
        return result.reshape(TOK_DEV, HW)

    attended = lax.map(one_device, jnp.arange(N_LOOP, dtype=jnp.int32)).reshape(TOKENS, HW)
    return jnp.dot(attended, out_weight, preferred_element_type=jnp.float32).astype(jnp.bfloat16)
```

```python
import functools
import math

import jax
import jax.numpy as jnp
from jax import lax
from jax.experimental import pallas as pl
from jax.experimental.pallas import tpu as pltpu
from jax.sharding import PartitionSpec as P

HD = 128
NEG = -1e30
ROWS = 256
FACTOR = HD**-0.5 * math.log2(math.e)
MESH = pl.DeviceIdType.MESH
F32 = jnp.float32
BF16 = jnp.bfloat16


def scores_of(q, k):
    return lax.dot_general(q, k, (((1,), (1,)), ((), ())), preferred_element_type=F32)


def with_ones(v):
    return jnp.concatenate([v, jnp.ones_like(v)], axis=1)


def row_bias(bias, first, count, length):
    rows = [
        jnp.broadcast_to(bias[first + i : first + i + 1, :], (length, bias.shape[1]))
        for i in range(count)
    ]
    return jnp.concatenate(rows, axis=0)


def pick_kernel(n, picks, wanted, pk, pv, send, sem):
    def copies(i):
        reader, pick = i // picks, i % picks
        block = wanted[i]
        return (
            pltpu.make_async_copy(pk.at[block], send.at[reader, 0, pick], sem.at[2 * i]),
            pltpu.make_async_copy(pv.at[block], send.at[reader, 1, pick], sem.at[2 * i + 1]),
        )

    @pl.loop(0, n * picks)
    def _(i):
        for c in copies(i):
            c.start()

    @pl.loop(0, n * picks)
    def _(i):
        for c in copies(i):
            c.wait()


def pick_blocks(wanted, pk, pv, n, picks):
    return pl.pallas_call(
        functools.partial(pick_kernel, n, picks),
        out_shape=jax.ShapeDtypeStruct((n, 2, picks) + pk.shape[1:], pk.dtype),
        in_specs=[
            pl.BlockSpec(memory_space=pltpu.SMEM),
            pl.BlockSpec(memory_space=pl.ANY),
            pl.BlockSpec(memory_space=pl.ANY),
        ],
        out_specs=pl.BlockSpec(memory_space=pl.ANY),
        scratch_shapes=[pltpu.SemaphoreType.DMA((2 * n * picks,))],
        name="pick",
    )(wanted, pk, pv)


def near_kernel(
    n, q, ck, cv, pk, pv, bias, ck_all, cv_all, send,
    acc, mx, tot, got, part, s_sem, r_sem, p_send, p_recv, own_sem,
):
    head = pl.program_id(0)
    me = lax.axis_index("loop")
    partner = me + 1 - 2 * lax.rem(me, 2)

    def to(dst):
        return pltpu.make_async_remote_copy(
            src_ref=send.at[dst], dst_ref=got.at[me], send_sem=s_sem.at[dst],
            recv_sem=r_sem.at[me], device_id={"loop": dst}, device_id_type=MESH,
        )

    def source(src):
        return pltpu.make_async_remote_copy(
            src_ref=send.at[src], dst_ref=got.at[src], send_sem=s_sem.at[src],
            recv_sem=r_sem.at[src], device_id={"loop": src}, device_id_type=MESH,
        )

    def half(i, ref):
        return pltpu.make_async_remote_copy(
            src_ref=ref, dst_ref=part.at[i], send_sem=p_send.at[i],
            recv_sem=p_recv.at[i], device_id={"loop": partner}, device_id_type=MESH,
        )

    own = pltpu.make_async_copy(send.at[me], got.at[me], own_sem)

    @pl.when(head == 0)
    def _():
        barrier = pltpu.get_barrier_semaphore()

        @pl.loop(1, n)
        def _(k):
            pl.semaphore_signal(
                barrier, inc=1, device_id={"loop": lax.rem(me + k, n)}, device_id_type=MESH
            )

        pl.semaphore_wait(barrier, n - 1)

        @pl.loop(1, n)
        def _(k):
            to(lax.rem(me + k, n)).start()

        half(0, ck_all).start()
        half(1, cv_all).start()
        own.start()

    tokens = q.shape[0]
    length = tokens // bias.shape[0]
    v_own, v_past = with_ones(cv[...]), with_ones(pv[...])
    for r in range(0, tokens, ROWS):
        qr = q[r : r + ROWS, :]
        s_own = scores_of(qr, ck[...]) + row_bias(bias, r // length, ROWS // length, length)
        s_past = scores_of(qr, pk[...])
        m = jnp.maximum(s_own.max(-1, keepdims=True), s_past.max(-1, keepdims=True)) * FACTOR
        w_own = jnp.exp2(s_own * FACTOR - m).astype(BF16)
        w_past = jnp.exp2(s_past * FACTOR - m).astype(BF16)
        out = jnp.dot(w_own, v_own, preferred_element_type=F32)
        out = out + jnp.dot(w_past, v_past, preferred_element_type=F32)
        acc[r : r + ROWS, :] = out[:, :HD]
        tot[r : r + ROWS, :] = out[:, HD:]
        mx[r : r + ROWS, :] = jnp.broadcast_to(m, (ROWS, HD))

    @pl.when(head == pl.num_programs(0) - 1)
    def _():
        @pl.loop(1, n)
        def _(k):
            to(lax.rem(me + k, n)).wait_send()
            source(lax.rem(me + k, n)).wait_recv()

        half(0, ck_all).wait()
        half(1, cv_all).wait()
        own.wait()


def near(q, ck, cv, pk, pv, bias, send, n):
    tokens, width = q.shape
    past = pk.shape[0]
    heads = width // HD

    def col(rows):
        return pl.BlockSpec((rows, HD), lambda h: (0, h))

    hbm = pl.BlockSpec(memory_space=pl.ANY)
    f32 = jax.ShapeDtypeStruct((tokens, width), F32)
    dma = pltpu.SemaphoreType.DMA
    return pl.pallas_call(
        functools.partial(near_kernel, n),
        grid=(heads,),
        out_shape=(
            f32, f32, f32,
            jax.ShapeDtypeStruct(send.shape, send.dtype),
            jax.ShapeDtypeStruct((2, tokens, width), BF16),
        ),
        in_specs=[col(tokens), col(tokens), col(tokens), col(past), col(past),
                  pl.BlockSpec(bias.shape, lambda h: (0, 0)), hbm, hbm, hbm],
        out_specs=(col(tokens), col(tokens), col(tokens), hbm, hbm),
        scratch_shapes=[dma((n,)), dma((n,)), dma((2,)), dma((2,)), dma],
        compiler_params=pltpu.CompilerParams(
            collective_id=0, has_side_effects=True, vmem_limit_bytes=32 * 2**20
        ),
        name="near",
    )(q, ck, cv, pk, pv, bias, ck, cv, send)


def far_kernel(picks, list_len, place, q, part, got, bias, acc, mx, tot, out):
    tokens = q.shape[0]
    length = tokens // bias.shape[0]
    k_half, v_half = part[0], with_ones(part[1])
    for r in range(0, tokens, ROWS):
        qr = q[r : r + ROWS, :]
        first, count = r // length, ROWS // length
        s_half = scores_of(qr, k_half) + row_bias(bias, first, count, length)
        s_list, v_list = [], []
        for b in range(first, first + count):
            places = [place[b * list_len + j] for j in range(list_len)]
            keys = [got[p // picks, 0, p % picks] for p in places]
            values = [got[p // picks, 1, p % picks] for p in places]
            s_list.append(
                scores_of(q[b * length : (b + 1) * length, :], jnp.concatenate(keys, axis=0))
            )
            v_list.append(with_ones(jnp.concatenate(values, axis=0)))
        s_far = jnp.concatenate(s_list, axis=0)
        m_old = mx[r : r + ROWS, :]
        m_new = jnp.maximum(s_half.max(-1, keepdims=True), s_far.max(-1, keepdims=True)) * FACTOR
        m = jnp.maximum(m_old, jnp.broadcast_to(m_new, m_old.shape))
        keep = jnp.exp2(m_old - m)
        m1 = m[:, :1]
        w_half = jnp.exp2(s_half * FACTOR - m1).astype(BF16)
        w_far = jnp.exp2(s_far * FACTOR - m1).astype(BF16)
        both = jnp.dot(w_half, v_half, preferred_element_type=F32)
        both = both + jnp.concatenate(
            [
                jnp.dot(w_far[i * length : (i + 1) * length], v, preferred_element_type=F32)
                for i, v in enumerate(v_list)
            ],
            axis=0,
        )
        total = tot[r : r + ROWS, :] * keep + both[:, HD:]
        mixed = acc[r : r + ROWS, :] * keep + both[:, :HD]
        out[r : r + ROWS, :] = (mixed / total).astype(out.dtype)


def far(place, q, part, got, bias, acc, mx, tot, list_len):
    tokens, width = q.shape
    n, _, picks, block_len, _ = got.shape

    def col(rows):
        return pl.BlockSpec((rows, HD), lambda h: (0, h))

    return pl.pallas_call(
        functools.partial(far_kernel, picks, list_len),
        grid=(width // HD,),
        out_shape=jax.ShapeDtypeStruct((tokens, width), BF16),
        in_specs=[
            pl.BlockSpec(memory_space=pltpu.SMEM),
            col(tokens),
            pl.BlockSpec((2, tokens, HD), lambda h: (0, 0, h)),
            pl.BlockSpec((n, 2, picks, block_len, HD), lambda h: (0, 0, 0, 0, h)),
            pl.BlockSpec(bias.shape, lambda h: (0, 0)),
            col(tokens), col(tokens), col(tokens),
        ],
        out_specs=col(tokens),
        compiler_params=pltpu.CompilerParams(vmem_limit_bytes=32 * 2**20),
        name="far",
    )(place, q, part, got, bias, acc, mx, tot)


def plan(pattern, read_blocks, past_count, length, n, me):
    blocks, list_len = pattern.shape[0], read_blocks.shape[1]
    entries = blocks * list_len
    picks = entries // n
    parity = me % 2
    own = lax.dynamic_slice_in_dim(pattern, parity * blocks, blocks, 1)
    other = lax.dynamic_slice_in_dim(pattern, (1 - parity) * blocks, blocks, 1)
    own = (own > 0) | (jnp.arange(blocks)[:, None] == jnp.arange(blocks)[None, :])
    bias = [
        jnp.repeat(jnp.where(o, 0.0, NEG).astype(F32), length, axis=1) for o in (own, other > 0)
    ]
    lists = read_blocks.reshape(n, entries)
    earlier = jnp.arange(entries)[None, :] < jnp.arange(entries)[:, None]
    mine = lists // past_count == me
    rank = jnp.sum(jnp.where(earlier[None], mine[:, None, :], False).astype(jnp.int32), axis=2)
    hit = mine[:, None, :] & (rank[:, None, :] == jnp.arange(picks)[None, :, None])
    wanted = jnp.sum(jnp.where(hit, (lists - me * past_count)[:, None, :], 0), axis=2)
    my_list = lax.dynamic_index_in_dim(lists, me, 0, keepdims=False) // past_count
    same = (my_list[None, :] == my_list[:, None]) & earlier
    place = my_list * picks + jnp.sum(same.astype(jnp.int32), axis=1)
    return bias[0], bias[1], wanted.reshape(-1).astype(jnp.int32), place.astype(jnp.int32)


def local(queries, cur_keys, cur_values, past_keys, past_values, pattern, read_blocks, out_weight):
    n = lax.axis_size("loop")
    me = lax.axis_index("loop")
    past_count, block_len, width = past_keys.shape
    length = queries.shape[0] // pattern.shape[0]
    list_len = read_blocks.shape[1]
    weight = lax.all_gather(out_weight, "loop", axis=0, tiled=True)
    bias_own, bias_other, wanted, place = plan(pattern, read_blocks, past_count, length, n, me)
    send = pick_blocks(wanted, past_keys, past_values, n, wanted.shape[0] // n)
    acc, mx, tot, got, part = near(
        queries, cur_keys, cur_values,
        past_keys.reshape(past_count * block_len, width),
        past_values.reshape(past_count * block_len, width),
        bias_own, send, n,
    )
    attended = far(place, queries, part, got, bias_other, acc, mx, tot, list_len)
    return jnp.dot(attended, weight, preferred_element_type=F32).astype(BF16)


def solution(mesh):
    return jax.shard_map(
        local,
        mesh=mesh,
        in_specs=(
            P(("groups", "loop"), None),
            P(("groups", "loop"), None),
            P(("groups", "loop"), None),
            P(("groups", "loop"), None, None),
            P(("groups", "loop"), None, None),
            P(("groups", "loop"), None),
            P("groups", None),
            P("loop", None),
        ),
        out_specs=P(("groups", "loop"), None),
        check_vma=False,
    )
```

```python
import functools
import math

import jax
import jax.numpy as jnp
from jax import lax
from jax.experimental import pallas as pl
from jax.experimental.pallas import tpu as pltpu
from jax.sharding import PartitionSpec as P

HD = 128
NEG = -1e30
ROWS = 256
FACTOR = HD**-0.5 * math.log2(math.e)
ROOM = 60 * 2**20
MESH = pl.DeviceIdType.MESH
F32 = jnp.float32
BF16 = jnp.bfloat16


def scores_of(q, k):
    return lax.dot_general(q, k, (((1,), (1,)), ((), ())), preferred_element_type=F32)


def with_ones(v):
    return jnp.concatenate([v, jnp.ones_like(v)], axis=1)


def row_bias(bias, first, count, length):
    rows = [
        jnp.broadcast_to(bias[first + i : first + i + 1, :], (length, bias.shape[1]))
        for i in range(count)
    ]
    return jnp.concatenate(rows, axis=0)


def pick_kernel(wanted, pk, pv, send):
    send[0, 0, 0] = pk[0]
    send[0, 1, 0] = pv[0]


def pick_blocks(wanted, pk, pv, n, picks):
    block = pl.BlockSpec((1,) + pk.shape[1:], lambda r, p, wanted: (wanted[r * picks + p], 0, 0))
    return pl.pallas_call(
        pick_kernel,
        out_shape=jax.ShapeDtypeStruct((n, 2, picks) + pk.shape[1:], pk.dtype),
        grid_spec=pltpu.PrefetchScalarGridSpec(
            num_scalar_prefetch=1,
            grid=(n, picks),
            in_specs=[block, block],
            out_specs=pl.BlockSpec(
                (1, 2, 1) + pk.shape[1:], lambda r, p, wanted: (r, 0, p, 0, 0)
            ),
        ),
        name="pick",
    )(wanted, pk, pv)


def near_kernel(
    n, q, ck, cv, pk, pv, bias, ck_all, cv_all, send,
    acc, mx, tot, got, part, s_sem, r_sem, p_send, p_recv, own_sem,
):
    head = pl.program_id(0)
    me = lax.axis_index("loop")
    partner = me + 1 - 2 * lax.rem(me, 2)

    def to(dst):
        return pltpu.make_async_remote_copy(
            src_ref=send.at[dst], dst_ref=got.at[me], send_sem=s_sem.at[dst],
            recv_sem=r_sem.at[me], device_id={"loop": dst}, device_id_type=MESH,
        )

    def source(src):
        return pltpu.make_async_remote_copy(
            src_ref=send.at[src], dst_ref=got.at[src], send_sem=s_sem.at[src],
            recv_sem=r_sem.at[src], device_id={"loop": src}, device_id_type=MESH,
        )

    def half(i, ref):
        return pltpu.make_async_remote_copy(
            src_ref=ref, dst_ref=part.at[i], send_sem=p_send.at[i],
            recv_sem=p_recv.at[i], device_id={"loop": partner}, device_id_type=MESH,
        )

    own = pltpu.make_async_copy(send.at[me], got.at[me], own_sem)

    @pl.when(head == 0)
    def _():
        barrier = pltpu.get_barrier_semaphore()

        @pl.loop(1, n)
        def _(k):
            pl.semaphore_signal(
                barrier, inc=1, device_id={"loop": lax.rem(me + k, n)}, device_id_type=MESH
            )

        pl.semaphore_wait(barrier, n - 1)

        @pl.loop(1, n)
        def _(k):
            to(lax.rem(me + k, n)).start()

        half(0, ck_all).start()
        half(1, cv_all).start()
        own.start()

    tokens = q.shape[0]
    length = tokens // bias.shape[0]
    v_own, v_past = with_ones(cv[...]), with_ones(pv[...])
    for r in range(0, tokens, ROWS):
        qr = q[r : r + ROWS, :]
        s_own = scores_of(qr, ck[...]) + row_bias(bias, r // length, ROWS // length, length)
        s_past = scores_of(qr, pk[...])
        m = jnp.maximum(s_own.max(-1, keepdims=True), s_past.max(-1, keepdims=True)) * FACTOR
        w_own = jnp.exp2(s_own * FACTOR - m).astype(BF16)
        w_past = jnp.exp2(s_past * FACTOR - m).astype(BF16)
        out = jnp.dot(w_own, v_own, preferred_element_type=F32)
        out = out + jnp.dot(w_past, v_past, preferred_element_type=F32)
        acc[r : r + ROWS, :] = out[:, :HD]
        tot[r : r + ROWS, :] = out[:, HD:]
        mx[r : r + ROWS, :] = jnp.broadcast_to(m, (ROWS, HD))

    @pl.when(head == pl.num_programs(0) - 1)
    def _():
        @pl.loop(1, n)
        def _(k):
            to(lax.rem(me + k, n)).wait_send()
            source(lax.rem(me + k, n)).wait_recv()

        half(0, ck_all).wait()
        half(1, cv_all).wait()
        own.wait()


def near(q, ck, cv, pk, pv, bias, send, n):
    tokens, width = q.shape
    past = pk.shape[0]
    heads = width // HD

    def col(rows):
        return pl.BlockSpec((rows, HD), lambda h: (0, h))

    hbm = pl.BlockSpec(memory_space=pl.ANY)
    f32 = jax.ShapeDtypeStruct((tokens, width), F32)
    dma = pltpu.SemaphoreType.DMA
    return pl.pallas_call(
        functools.partial(near_kernel, n),
        grid=(heads,),
        out_shape=(
            f32, f32, f32,
            jax.ShapeDtypeStruct(send.shape, send.dtype),
            jax.ShapeDtypeStruct((2, tokens, width), BF16),
        ),
        in_specs=[col(tokens), col(tokens), col(tokens), col(past), col(past),
                  pl.BlockSpec(bias.shape, lambda h: (0, 0)), hbm, hbm, hbm],
        out_specs=(col(tokens), col(tokens), col(tokens), hbm, hbm),
        scratch_shapes=[dma((n,)), dma((n,)), dma((2,)), dma((2,)), dma],
        compiler_params=pltpu.CompilerParams(
            collective_id=0, has_side_effects=True, vmem_limit_bytes=ROOM
        ),
        cost_estimate=pl.CostEstimate(
            flops=60 * tokens * (tokens + past) * width,
            bytes_accessed=40 * tokens * width,
            transcendentals=tokens * (tokens + past) * heads,
        ),
        name="near",
    )(q, ck, cv, pk, pv, bias, ck, cv, send)


def far_kernel(picks, list_len, place, q, part, got, bias, acc, mx, tot, out):
    tokens = q.shape[0]
    length = tokens // bias.shape[0]
    k_half, v_half = part[0], with_ones(part[1])
    for r in range(0, tokens, ROWS):
        qr = q[r : r + ROWS, :]
        first, count = r // length, ROWS // length
        s_half = scores_of(qr, k_half) + row_bias(bias, first, count, length)
        s_list, v_list = [], []
        for b in range(first, first + count):
            places = [place[b * list_len + j] for j in range(list_len)]
            keys = [got[p // picks, 0, p % picks] for p in places]
            values = [got[p // picks, 1, p % picks] for p in places]
            s_list.append(
                scores_of(q[b * length : (b + 1) * length, :], jnp.concatenate(keys, axis=0))
            )
            v_list.append(with_ones(jnp.concatenate(values, axis=0)))
        s_far = jnp.concatenate(s_list, axis=0)
        m_old = mx[r : r + ROWS, :]
        m_new = jnp.maximum(s_half.max(-1, keepdims=True), s_far.max(-1, keepdims=True)) * FACTOR
        m = jnp.maximum(m_old, jnp.broadcast_to(m_new, m_old.shape))
        keep = jnp.exp2(m_old - m)
        m1 = m[:, :1]
        w_half = jnp.exp2(s_half * FACTOR - m1).astype(BF16)
        w_far = jnp.exp2(s_far * FACTOR - m1).astype(BF16)
        both = jnp.dot(w_half, v_half, preferred_element_type=F32)
        both = both + jnp.concatenate(
            [
                jnp.dot(w_far[i * length : (i + 1) * length], v, preferred_element_type=F32)
                for i, v in enumerate(v_list)
            ],
            axis=0,
        )
        total = tot[r : r + ROWS, :] * keep + both[:, HD:]
        mixed = acc[r : r + ROWS, :] * keep + both[:, :HD]
        out[r : r + ROWS, :] = (mixed / total).astype(out.dtype)


def far(place, q, part, got, bias, acc, mx, tot, list_len):
    tokens, width = q.shape
    n, _, picks, block_len, _ = got.shape

    def col(rows):
        return pl.BlockSpec((rows, HD), lambda h: (0, h))

    return pl.pallas_call(
        functools.partial(far_kernel, picks, list_len),
        grid=(width // HD,),
        out_shape=jax.ShapeDtypeStruct((tokens, width), BF16),
        in_specs=[
            pl.BlockSpec(memory_space=pltpu.SMEM),
            col(tokens),
            pl.BlockSpec((2, tokens, HD), lambda h: (0, 0, h)),
            pl.BlockSpec((n, 2, picks, block_len, HD), lambda h: (0, 0, 0, 0, h)),
            pl.BlockSpec(bias.shape, lambda h: (0, 0)),
            col(tokens), col(tokens), col(tokens),
        ],
        out_specs=col(tokens),
        compiler_params=pltpu.CompilerParams(vmem_limit_bytes=ROOM),
        cost_estimate=pl.CostEstimate(
            flops=12 * tokens * tokens * width,
            bytes_accessed=30 * tokens * width,
            transcendentals=2 * tokens * tokens * (width // HD),
        ),
        name="far",
    )(place, q, part, got, bias, acc, mx, tot)


def plan(pattern, read_blocks, past_count, length, n, me):
    blocks, list_len = pattern.shape[0], read_blocks.shape[1]
    entries = blocks * list_len
    picks = entries // n
    parity = me % 2
    own = lax.dynamic_slice_in_dim(pattern, parity * blocks, blocks, 1)
    other = lax.dynamic_slice_in_dim(pattern, (1 - parity) * blocks, blocks, 1)
    own = (own > 0) | (jnp.arange(blocks)[:, None] == jnp.arange(blocks)[None, :])
    bias = [
        jnp.repeat(jnp.where(o, 0.0, NEG).astype(F32), length, axis=1) for o in (own, other > 0)
    ]
    lists = read_blocks.reshape(n, entries)
    earlier = jnp.arange(entries)[None, :] < jnp.arange(entries)[:, None]
    mine = lists // past_count == me
    rank = jnp.sum(jnp.where(earlier[None], mine[:, None, :], False).astype(jnp.int32), axis=2)
    hit = mine[:, None, :] & (rank[:, None, :] == jnp.arange(picks)[None, :, None])
    wanted = jnp.sum(jnp.where(hit, (lists - me * past_count)[:, None, :], 0), axis=2)
    my_list = lax.dynamic_index_in_dim(lists, me, 0, keepdims=False) // past_count
    same = (my_list[None, :] == my_list[:, None]) & earlier
    place = my_list * picks + jnp.sum(same.astype(jnp.int32), axis=1)
    return bias[0], bias[1], wanted.reshape(-1).astype(jnp.int32), place.astype(jnp.int32)


def project_kernel(side, attended, weight, *rest):
    rest[-1][...] = jnp.dot(
        attended[...], weight[...], preferred_element_type=F32
    ).astype(BF16)


def project(side, attended, weight, done, tile):
    tokens, width = attended.shape
    columns = weight.shape[1]
    tiles = columns // tile
    more = [] if done is None else [done]
    return pl.pallas_call(
        project_kernel,
        out_shape=jax.ShapeDtypeStruct((tokens, 2 * columns), BF16),
        grid_spec=pltpu.PrefetchScalarGridSpec(
            num_scalar_prefetch=1,
            grid=(tiles,),
            in_specs=[
                pl.BlockSpec((tokens, width), lambda t, side: (0, 0)),
                pl.BlockSpec((width, tile), lambda t, side: (0, t)),
            ]
            + [pl.BlockSpec(memory_space=pl.ANY)] * len(more),
            out_specs=pl.BlockSpec((tokens, tile), lambda t, side: (0, side[0] * tiles + t)),
        ),
        input_output_aliases={} if done is None else {3: 0},
        compiler_params=pltpu.CompilerParams(vmem_limit_bytes=ROOM),
        cost_estimate=pl.CostEstimate(
            flops=2 * tokens * width * columns,
            bytes_accessed=2 * (width * columns + tokens * (width + columns)),
            transcendentals=0,
        ),
        name="project",
    )(side, attended, weight, *more)


def swap_cores(value, n):
    return lax.ppermute(value, "loop", [(i, i ^ 1) for i in range(n)])


def gather_half(out_weight, n, me):
    half = out_weight.shape[1] // 2
    parity = me % 2
    mine = lax.dynamic_slice_in_dim(out_weight, parity * half, half, 1)
    its = swap_cores(lax.dynamic_slice_in_dim(out_weight, (1 - parity) * half, half, 1), n)
    rows = jnp.concatenate(
        [jnp.where(parity == 0, mine, its), jnp.where(parity == 0, its, mine)], axis=0
    )
    groups = [list(range(c, n, 2)) for c in range(2)]
    return lax.all_gather(rows, "loop", axis=0, tiled=True, axis_index_groups=groups)


def local(queries, cur_keys, cur_values, past_keys, past_values, pattern, read_blocks, out_weight):
    n = lax.axis_size("loop")
    me = lax.axis_index("loop")
    past_count, block_len, width = past_keys.shape
    length = queries.shape[0] // pattern.shape[0]
    list_len = read_blocks.shape[1]
    my_half = gather_half(out_weight, n, me)
    bias_own, bias_other, wanted, place = plan(pattern, read_blocks, past_count, length, n, me)
    send = pick_blocks(wanted, past_keys, past_values, n, wanted.shape[0] // n)
    acc, mx, tot, got, part = near(
        queries, cur_keys, cur_values,
        past_keys.reshape(past_count * block_len, width),
        past_values.reshape(past_count * block_len, width),
        bias_own, send, n,
    )
    my_half, got = lax.optimization_barrier((my_half, got))
    attended = far(place, queries, part, got, bias_other, acc, mx, tot, list_len)
    its_half = swap_cores(my_half, n)
    side = (me % 2).astype(jnp.int32).reshape(1)
    done = project(side, attended, my_half, None, 512)
    return project(1 - side, attended, its_half, done, 512)


def solution(mesh):
    return jax.shard_map(
        local,
        mesh=mesh,
        in_specs=(
            P(("groups", "loop"), None),
            P(("groups", "loop"), None),
            P(("groups", "loop"), None),
            P(("groups", "loop"), None, None),
            P(("groups", "loop"), None, None),
            P(("groups", "loop"), None),
            P("groups", None),
            P("loop", None),
        ),
        out_specs=P(("groups", "loop"), None),
        check_vma=False,
    )
```

```python
import functools
import math

import jax
import jax.numpy as jnp
from jax import lax
from jax.experimental import pallas as pl
from jax.experimental.pallas import tpu as pltpu
from jax.sharding import PartitionSpec as P

HD = 128
NEG = -1e30
ROWS = 256
FACTOR = HD**-0.5 * math.log2(math.e)
ROOM = 60 * 2**20
MESH = pl.DeviceIdType.MESH
F32 = jnp.float32
BF16 = jnp.bfloat16


def scores_of(q, k):
    return lax.dot_general(q, k, (((1,), (1,)), ((), ())), preferred_element_type=F32)


def with_ones(v):
    return jnp.concatenate([v, jnp.ones_like(v)], axis=1)


def row_bias(bias, first, count, length):
    rows = [
        jnp.broadcast_to(bias[first + i : first + i + 1, :], (length, bias.shape[1]))
        for i in range(count)
    ]
    return jnp.concatenate(rows, axis=0)


def pick_kernel(wanted, pk, pv, send):
    send[0, 0, 0] = pk[0]
    send[0, 1, 0] = pv[0]


def pick_blocks(wanted, pk, pv, n, picks):
    block = pl.BlockSpec((1,) + pk.shape[1:], lambda r, p, wanted: (wanted[r * picks + p], 0, 0))
    return pl.pallas_call(
        pick_kernel,
        out_shape=jax.ShapeDtypeStruct((n, 2, picks) + pk.shape[1:], pk.dtype),
        grid_spec=pltpu.PrefetchScalarGridSpec(
            num_scalar_prefetch=1,
            grid=(n, picks),
            in_specs=[block, block],
            out_specs=pl.BlockSpec(
                (1, 2, 1) + pk.shape[1:], lambda r, p, wanted: (r, 0, p, 0, 0)
            ),
        ),
        name="pick",
    )(wanted, pk, pv)


def near_kernel(
    n, q, ck, cv, pk, pv, bias, ck_all, cv_all, send,
    acc, mx, tot, got, part, s_sem, r_sem, p_send, p_recv, own_sem,
):
    head = pl.program_id(0)
    me = lax.axis_index("loop")
    partner = me + 1 - 2 * lax.rem(me, 2)

    def to(dst):
        return pltpu.make_async_remote_copy(
            src_ref=send.at[dst], dst_ref=got.at[me], send_sem=s_sem.at[dst],
            recv_sem=r_sem.at[me], device_id={"loop": dst}, device_id_type=MESH,
        )

    def source(src):
        return pltpu.make_async_remote_copy(
            src_ref=send.at[src], dst_ref=got.at[src], send_sem=s_sem.at[src],
            recv_sem=r_sem.at[src], device_id={"loop": src}, device_id_type=MESH,
        )

    def half(i, ref):
        return pltpu.make_async_remote_copy(
            src_ref=ref, dst_ref=part.at[i], send_sem=p_send.at[i],
            recv_sem=p_recv.at[i], device_id={"loop": partner}, device_id_type=MESH,
        )

    own = pltpu.make_async_copy(send.at[me], got.at[me], own_sem)

    @pl.when(head == 0)
    def _():
        barrier = pltpu.get_barrier_semaphore()

        @pl.loop(1, n)
        def _(k):
            pl.semaphore_signal(
                barrier, inc=1, device_id={"loop": lax.rem(me + k, n)}, device_id_type=MESH
            )

        pl.semaphore_wait(barrier, n - 1)

        @pl.loop(1, n)
        def _(k):
            to(lax.rem(me + k, n)).start()

        half(0, ck_all).start()
        half(1, cv_all).start()
        own.start()

    tokens = q.shape[0]
    length = tokens // bias.shape[0]
    v_own, v_past = with_ones(cv[...]), with_ones(pv[...])
    for r in range(0, tokens, ROWS):
        qr = q[r : r + ROWS, :]
        s_own = scores_of(qr, ck[...]) + row_bias(bias, r // length, ROWS // length, length)
        s_past = scores_of(qr, pk[...])
        m = jnp.maximum(s_own.max(-1, keepdims=True), s_past.max(-1, keepdims=True)) * FACTOR
        w_own = jnp.exp2(s_own * FACTOR - m).astype(BF16)
        w_past = jnp.exp2(s_past * FACTOR - m).astype(BF16)
        out = jnp.dot(w_own, v_own, preferred_element_type=F32)
        out = out + jnp.dot(w_past, v_past, preferred_element_type=F32)
        acc[r : r + ROWS, :] = out[:, :HD]
        tot[r : r + ROWS, :] = out[:, HD:]
        mx[r : r + ROWS, :] = jnp.broadcast_to(m, (ROWS, HD))

    @pl.when(head == pl.num_programs(0) - 1)
    def _():
        @pl.loop(1, n)
        def _(k):
            to(lax.rem(me + k, n)).wait_send()
            source(lax.rem(me + k, n)).wait_recv()

        half(0, ck_all).wait()
        half(1, cv_all).wait()
        own.wait()


def near(q, ck, cv, pk, pv, bias, send, n):
    tokens, width = q.shape
    past = pk.shape[0]
    heads = width // HD

    def col(rows):
        return pl.BlockSpec((rows, HD), lambda h: (0, h))

    hbm = pl.BlockSpec(memory_space=pl.ANY)
    f32 = jax.ShapeDtypeStruct((tokens, width), F32)
    dma = pltpu.SemaphoreType.DMA
    return pl.pallas_call(
        functools.partial(near_kernel, n),
        grid=(heads,),
        out_shape=(
            f32, f32, f32,
            jax.ShapeDtypeStruct(send.shape, send.dtype),
            jax.ShapeDtypeStruct((2, tokens, width), BF16),
        ),
        in_specs=[col(tokens), col(tokens), col(tokens), col(past), col(past),
                  pl.BlockSpec(bias.shape, lambda h: (0, 0)), hbm, hbm, hbm],
        out_specs=(col(tokens), col(tokens), col(tokens), hbm, hbm),
        scratch_shapes=[dma((n,)), dma((n,)), dma((2,)), dma((2,)), dma],
        compiler_params=pltpu.CompilerParams(
            collective_id=0, has_side_effects=True, vmem_limit_bytes=ROOM
        ),
        cost_estimate=pl.CostEstimate(
            flops=60 * tokens * (tokens + past) * width,
            bytes_accessed=40 * tokens * width,
            transcendentals=tokens * (tokens + past) * heads,
        ),
        name="near",
    )(q, ck, cv, pk, pv, bias, ck, cv, send)


def far_kernel(picks, list_len, place, q, part, got, bias, acc, mx, tot, out):
    tokens = q.shape[0]
    length = tokens // bias.shape[0]
    k_half, v_half = part[0], with_ones(part[1])
    for r in range(0, tokens, ROWS):
        qr = q[r : r + ROWS, :]
        first, count = r // length, ROWS // length
        s_half = scores_of(qr, k_half) + row_bias(bias, first, count, length)
        s_list, v_list = [], []
        for b in range(first, first + count):
            places = [place[b * list_len + j] for j in range(list_len)]
            keys = [got[p // picks, 0, p % picks] for p in places]
            values = [got[p // picks, 1, p % picks] for p in places]
            s_list.append(
                scores_of(q[b * length : (b + 1) * length, :], jnp.concatenate(keys, axis=0))
            )
            v_list.append(with_ones(jnp.concatenate(values, axis=0)))
        s_far = jnp.concatenate(s_list, axis=0)
        m_old = mx[r : r + ROWS, :]
        m_new = jnp.maximum(s_half.max(-1, keepdims=True), s_far.max(-1, keepdims=True)) * FACTOR
        m = jnp.maximum(m_old, jnp.broadcast_to(m_new, m_old.shape))
        keep = jnp.exp2(m_old - m)
        m1 = m[:, :1]
        w_half = jnp.exp2(s_half * FACTOR - m1).astype(BF16)
        w_far = jnp.exp2(s_far * FACTOR - m1).astype(BF16)
        both = jnp.dot(w_half, v_half, preferred_element_type=F32)
        both = both + jnp.concatenate(
            [
                jnp.dot(w_far[i * length : (i + 1) * length], v, preferred_element_type=F32)
                for i, v in enumerate(v_list)
            ],
            axis=0,
        )
        total = tot[r : r + ROWS, :] * keep + both[:, HD:]
        mixed = acc[r : r + ROWS, :] * keep + both[:, :HD]
        out[r : r + ROWS, :] = (mixed / total).astype(out.dtype)


def far(place, q, part, got, bias, acc, mx, tot, list_len):
    tokens, width = q.shape
    n, _, picks, block_len, _ = got.shape

    def col(rows):
        return pl.BlockSpec((rows, HD), lambda h: (0, h))

    return pl.pallas_call(
        functools.partial(far_kernel, picks, list_len),
        grid=(width // HD,),
        out_shape=jax.ShapeDtypeStruct((tokens, width), BF16),
        in_specs=[
            pl.BlockSpec(memory_space=pltpu.SMEM),
            col(tokens),
            pl.BlockSpec((2, tokens, HD), lambda h: (0, 0, h)),
            pl.BlockSpec((n, 2, picks, block_len, HD), lambda h: (0, 0, 0, 0, h)),
            pl.BlockSpec(bias.shape, lambda h: (0, 0)),
            col(tokens), col(tokens), col(tokens),
        ],
        out_specs=col(tokens),
        compiler_params=pltpu.CompilerParams(vmem_limit_bytes=ROOM),
        cost_estimate=pl.CostEstimate(
            flops=12 * tokens * tokens * width,
            bytes_accessed=30 * tokens * width,
            transcendentals=2 * tokens * tokens * (width // HD),
        ),
        name="far",
    )(place, q, part, got, bias, acc, mx, tot)


def plan(pattern, read_blocks, past_count, length, n, me):
    blocks, list_len = pattern.shape[0], read_blocks.shape[1]
    entries = blocks * list_len
    picks = entries // n
    parity = me % 2
    own = lax.dynamic_slice_in_dim(pattern, parity * blocks, blocks, 1)
    other = lax.dynamic_slice_in_dim(pattern, (1 - parity) * blocks, blocks, 1)
    own = (own > 0) | (jnp.arange(blocks)[:, None] == jnp.arange(blocks)[None, :])
    bias = [
        jnp.repeat(jnp.where(o, 0.0, NEG).astype(F32), length, axis=1) for o in (own, other > 0)
    ]
    lists = read_blocks.reshape(n, entries)
    earlier = jnp.arange(entries)[None, :] < jnp.arange(entries)[:, None]
    mine = lists // past_count == me
    rank = jnp.sum(jnp.where(earlier[None], mine[:, None, :], False).astype(jnp.int32), axis=2)
    hit = mine[:, None, :] & (rank[:, None, :] == jnp.arange(picks)[None, :, None])
    wanted = jnp.sum(jnp.where(hit, (lists - me * past_count)[:, None, :], 0), axis=2)
    my_list = lax.dynamic_index_in_dim(lists, me, 0, keepdims=False) // past_count
    same = (my_list[None, :] == my_list[:, None]) & earlier
    place = my_list * picks + jnp.sum(same.astype(jnp.int32), axis=1)
    return bias[0], bias[1], wanted.reshape(-1).astype(jnp.int32), place.astype(jnp.int32)


def project_kernel(first, attended, weight, *rest):
    rest[-1][...] = jnp.dot(
        attended[...], weight[...], preferred_element_type=F32
    ).astype(BF16)


def project(first, attended, weight, done, whole, tile):
    tokens, width = attended.shape
    columns = weight.shape[1]
    more = [] if done is None else [done]
    return pl.pallas_call(
        project_kernel,
        out_shape=jax.ShapeDtypeStruct((tokens, whole), BF16),
        grid_spec=pltpu.PrefetchScalarGridSpec(
            num_scalar_prefetch=1,
            grid=(columns // tile,),
            in_specs=[
                pl.BlockSpec((tokens, width), lambda t, first: (0, 0)),
                pl.BlockSpec((width, tile), lambda t, first: (0, t)),
            ]
            + [pl.BlockSpec(memory_space=pl.ANY)] * len(more),
            out_specs=pl.BlockSpec((tokens, tile), lambda t, first: (0, first[0] + t)),
        ),
        input_output_aliases={} if done is None else {3: 0},
        compiler_params=pltpu.CompilerParams(vmem_limit_bytes=ROOM),
        cost_estimate=pl.CostEstimate(
            flops=2 * tokens * width * columns,
            bytes_accessed=2 * (width * columns + tokens * (width + columns)),
            transcendentals=0,
        ),
        name="project",
    )(first.astype(jnp.int32).reshape(1), attended, weight, *more)


def local(queries, cur_keys, cur_values, past_keys, past_values, pattern, read_blocks, out_weight):
    n = lax.axis_size("loop")
    groups = lax.axis_size("groups")
    me = lax.axis_index("loop")
    side = lax.axis_index("groups") % 2
    past_count, block_len, width = past_keys.shape
    length = queries.shape[0] // pattern.shape[0]
    list_len = read_blocks.shape[1]
    whole = out_weight.shape[1]
    piece = whole // 5
    tile = piece // 2
    mine = lax.all_gather(
        lax.dynamic_slice_in_dim(out_weight, side * piece, piece, 1), "loop", axis=0, tiled=True
    )
    rest = lax.all_gather(out_weight[:, 2 * piece :], "loop", axis=0, tiled=True)
    bias_own, bias_other, wanted, place = plan(pattern, read_blocks, past_count, length, n, me)
    send = pick_blocks(wanted, past_keys, past_values, n, wanted.shape[0] // n)
    mine, send = lax.optimization_barrier((mine, send))
    its = lax.ppermute(mine, "groups", [(i, i ^ 1) for i in range(groups)])
    acc, mx, tot, got, part = near(
        queries, cur_keys, cur_values,
        past_keys.reshape(past_count * block_len, width),
        past_values.reshape(past_count * block_len, width),
        bias_own, send, n,
    )
    attended = far(place, queries, part, got, bias_other, acc, mx, tot, list_len)
    done = project(2 * side, attended, mine, None, whole, tile)
    done = project(2 - 2 * side, attended, its, done, whole, tile)
    return project(jnp.full((), 4), attended, rest, done, whole, tile)


def solution(mesh):
    return jax.shard_map(
        local,
        mesh=mesh,
        in_specs=(
            P(("groups", "loop"), None),
            P(("groups", "loop"), None),
            P(("groups", "loop"), None),
            P(("groups", "loop"), None, None),
            P(("groups", "loop"), None, None),
            P(("groups", "loop"), None),
            P("groups", None),
            P("loop", None),
        ),
        out_specs=P(("groups", "loop"), None),
        check_vma=False,
    )
```

```python
import functools
import math

import jax
import jax.numpy as jnp
from jax import lax
from jax.experimental import pallas as pl
from jax.experimental.pallas import tpu as pltpu
from jax.sharding import PartitionSpec as P

HD = 128
NEG = -1e30
ROWS = 256
FACTOR = HD**-0.5 * math.log2(math.e)
ROOM = 60 * 2**20
MESH = pl.DeviceIdType.MESH
F32 = jnp.float32
BF16 = jnp.bfloat16


def scores_of(q, k):
    return lax.dot_general(q, k, (((1,), (1,)), ((), ())), preferred_element_type=F32)


def with_ones(v):
    return jnp.concatenate([v, jnp.ones_like(v)], axis=1)


def row_bias(bias, first, count, length):
    rows = [
        jnp.broadcast_to(bias[first + i : first + i + 1, :], (length, bias.shape[1]))
        for i in range(count)
    ]
    return jnp.concatenate(rows, axis=0)


def pick_kernel(wanted, pk, pv, send):
    send[0, 0, 0] = pk[0]
    send[0, 1, 0] = pv[0]


def pick_blocks(wanted, pk, pv, n, picks):
    block = pl.BlockSpec((1,) + pk.shape[1:], lambda r, p, wanted: (wanted[r * picks + p], 0, 0))
    return pl.pallas_call(
        pick_kernel,
        out_shape=jax.ShapeDtypeStruct((n, 2, picks) + pk.shape[1:], pk.dtype),
        grid_spec=pltpu.PrefetchScalarGridSpec(
            num_scalar_prefetch=1,
            grid=(n, picks),
            in_specs=[block, block],
            out_specs=pl.BlockSpec(
                (1, 2, 1) + pk.shape[1:], lambda r, p, wanted: (r, 0, p, 0, 0)
            ),
        ),
        name="pick",
    )(wanted, pk, pv)


def near_kernel(
    n, q, ck, cv, pk, pv, bias, ck_all, cv_all, send,
    acc, mx, tot, got, part, s_sem, r_sem, p_send, p_recv, own_sem,
):
    head = pl.program_id(0)
    me = lax.axis_index("loop")
    partner = me + 1 - 2 * lax.rem(me, 2)

    def to(dst):
        return pltpu.make_async_remote_copy(
            src_ref=send.at[dst], dst_ref=got.at[me], send_sem=s_sem.at[dst],
            recv_sem=r_sem.at[me], device_id={"loop": dst}, device_id_type=MESH,
        )

    def source(src):
        return pltpu.make_async_remote_copy(
            src_ref=send.at[src], dst_ref=got.at[src], send_sem=s_sem.at[src],
            recv_sem=r_sem.at[src], device_id={"loop": src}, device_id_type=MESH,
        )

    def half(i, ref):
        return pltpu.make_async_remote_copy(
            src_ref=ref, dst_ref=part.at[i], send_sem=p_send.at[i],
            recv_sem=p_recv.at[i], device_id={"loop": partner}, device_id_type=MESH,
        )

    own = pltpu.make_async_copy(send.at[me], got.at[me], own_sem)

    @pl.when(head == 0)
    def _():
        barrier = pltpu.get_barrier_semaphore()

        @pl.loop(1, n)
        def _(k):
            pl.semaphore_signal(
                barrier, inc=1, device_id={"loop": lax.rem(me + k, n)}, device_id_type=MESH
            )

        pl.semaphore_wait(barrier, n - 1)

        @pl.loop(1, n)
        def _(k):
            to(lax.rem(me + k, n)).start()

        half(0, ck_all).start()
        half(1, cv_all).start()
        own.start()

    tokens = q.shape[0]
    length = tokens // bias.shape[0]
    v_own, v_past = with_ones(cv[...]), with_ones(pv[...])
    for r in range(0, tokens, ROWS):
        qr = q[r : r + ROWS, :]
        s_own = scores_of(qr, ck[...]) + row_bias(bias, r // length, ROWS // length, length)
        s_past = scores_of(qr, pk[...])
        m = jnp.maximum(s_own.max(-1, keepdims=True), s_past.max(-1, keepdims=True)) * FACTOR
        w_own = jnp.exp2(s_own * FACTOR - m).astype(BF16)
        w_past = jnp.exp2(s_past * FACTOR - m).astype(BF16)
        out = jnp.dot(w_own, v_own, preferred_element_type=F32)
        out = out + jnp.dot(w_past, v_past, preferred_element_type=F32)
        acc[r : r + ROWS, :] = out[:, :HD]
        tot[r : r + ROWS, :] = out[:, HD:]
        mx[r : r + ROWS, :] = jnp.broadcast_to(m, (ROWS, HD))

    @pl.when(head == pl.num_programs(0) - 1)
    def _():
        @pl.loop(1, n)
        def _(k):
            to(lax.rem(me + k, n)).wait_send()
            source(lax.rem(me + k, n)).wait_recv()

        half(0, ck_all).wait()
        half(1, cv_all).wait()
        own.wait()


def near(q, ck, cv, pk, pv, bias, send, n):
    tokens, width = q.shape
    past = pk.shape[0]
    heads = width // HD

    def col(rows):
        return pl.BlockSpec((rows, HD), lambda h: (0, h))

    hbm = pl.BlockSpec(memory_space=pl.ANY)
    f32 = jax.ShapeDtypeStruct((tokens, width), F32)
    dma = pltpu.SemaphoreType.DMA
    return pl.pallas_call(
        functools.partial(near_kernel, n),
        grid=(heads,),
        out_shape=(
            f32, f32, f32,
            jax.ShapeDtypeStruct(send.shape, send.dtype),
            jax.ShapeDtypeStruct((2, tokens, width), BF16),
        ),
        in_specs=[col(tokens), col(tokens), col(tokens), col(past), col(past),
                  pl.BlockSpec(bias.shape, lambda h: (0, 0)), hbm, hbm, hbm],
        out_specs=(col(tokens), col(tokens), col(tokens), hbm, hbm),
        scratch_shapes=[dma((n,)), dma((n,)), dma((2,)), dma((2,)), dma],
        compiler_params=pltpu.CompilerParams(
            collective_id=0, has_side_effects=True, vmem_limit_bytes=ROOM
        ),
        cost_estimate=pl.CostEstimate(
            flops=60 * tokens * (tokens + past) * width,
            bytes_accessed=40 * tokens * width,
            transcendentals=tokens * (tokens + past) * heads,
        ),
        name="near",
    )(q, ck, cv, pk, pv, bias, ck, cv, send)


def far_kernel(picks, list_len, place, q, part, got, bias, acc, mx, tot, out):
    tokens = q.shape[0]
    length = tokens // bias.shape[0]
    k_half, v_half = part[0], with_ones(part[1])
    for r in range(0, tokens, ROWS):
        qr = q[r : r + ROWS, :]
        first, count = r // length, ROWS // length
        s_half = scores_of(qr, k_half) + row_bias(bias, first, count, length)
        s_list, v_list = [], []
        for b in range(first, first + count):
            places = [place[b * list_len + j] for j in range(list_len)]
            keys = [got[p // picks, 0, p % picks] for p in places]
            values = [got[p // picks, 1, p % picks] for p in places]
            s_list.append(
                scores_of(q[b * length : (b + 1) * length, :], jnp.concatenate(keys, axis=0))
            )
            v_list.append(with_ones(jnp.concatenate(values, axis=0)))
        s_far = jnp.concatenate(s_list, axis=0)
        m_old = mx[r : r + ROWS, :]
        m_new = jnp.maximum(s_half.max(-1, keepdims=True), s_far.max(-1, keepdims=True)) * FACTOR
        m = jnp.maximum(m_old, jnp.broadcast_to(m_new, m_old.shape))
        keep = jnp.exp2(m_old - m)
        m1 = m[:, :1]
        w_half = jnp.exp2(s_half * FACTOR - m1).astype(BF16)
        w_far = jnp.exp2(s_far * FACTOR - m1).astype(BF16)
        both = jnp.dot(w_half, v_half, preferred_element_type=F32)
        both = both + jnp.concatenate(
            [
                jnp.dot(w_far[i * length : (i + 1) * length], v, preferred_element_type=F32)
                for i, v in enumerate(v_list)
            ],
            axis=0,
        )
        total = tot[r : r + ROWS, :] * keep + both[:, HD:]
        mixed = acc[r : r + ROWS, :] * keep + both[:, :HD]
        out[r : r + ROWS, :] = (mixed / total).astype(out.dtype)


def far(place, q, part, got, bias, acc, mx, tot, list_len):
    tokens, width = q.shape
    n, _, picks, block_len, _ = got.shape

    def col(rows):
        return pl.BlockSpec((rows, HD), lambda h: (0, h))

    return pl.pallas_call(
        functools.partial(far_kernel, picks, list_len),
        grid=(width // HD,),
        out_shape=jax.ShapeDtypeStruct((tokens, width), BF16),
        in_specs=[
            pl.BlockSpec(memory_space=pltpu.SMEM),
            col(tokens),
            pl.BlockSpec((2, tokens, HD), lambda h: (0, 0, h)),
            pl.BlockSpec((n, 2, picks, block_len, HD), lambda h: (0, 0, 0, 0, h)),
            pl.BlockSpec(bias.shape, lambda h: (0, 0)),
            col(tokens), col(tokens), col(tokens),
        ],
        out_specs=col(tokens),
        compiler_params=pltpu.CompilerParams(vmem_limit_bytes=ROOM),
        cost_estimate=pl.CostEstimate(
            flops=12 * tokens * tokens * width,
            bytes_accessed=30 * tokens * width,
            transcendentals=2 * tokens * tokens * (width // HD),
        ),
        name="far",
    )(place, q, part, got, bias, acc, mx, tot)


def plan(pattern, read_blocks, past_count, length, n, me):
    blocks, list_len = pattern.shape[0], read_blocks.shape[1]
    entries = blocks * list_len
    picks = entries // n
    parity = me % 2
    own = lax.dynamic_slice_in_dim(pattern, parity * blocks, blocks, 1)
    other = lax.dynamic_slice_in_dim(pattern, (1 - parity) * blocks, blocks, 1)
    own = (own > 0) | (jnp.arange(blocks)[:, None] == jnp.arange(blocks)[None, :])
    bias = [
        jnp.repeat(jnp.where(o, 0.0, NEG).astype(F32), length, axis=1) for o in (own, other > 0)
    ]
    lists = read_blocks.reshape(n, entries)
    earlier = jnp.arange(entries)[None, :] < jnp.arange(entries)[:, None]
    mine = lists // past_count == me
    rank = jnp.sum(jnp.where(earlier[None], mine[:, None, :], False).astype(jnp.int32), axis=2)
    hit = mine[:, None, :] & (rank[:, None, :] == jnp.arange(picks)[None, :, None])
    wanted = jnp.sum(jnp.where(hit, (lists - me * past_count)[:, None, :], 0), axis=2)
    my_list = lax.dynamic_index_in_dim(lists, me, 0, keepdims=False) // past_count
    same = (my_list[None, :] == my_list[:, None]) & earlier
    place = my_list * picks + jnp.sum(same.astype(jnp.int32), axis=1)
    return bias[0], bias[1], wanted.reshape(-1).astype(jnp.int32), place.astype(jnp.int32)


def project_kernel(first, attended, weight, *rest):
    rest[-1][...] = jnp.dot(
        attended[...], weight[...], preferred_element_type=F32
    ).astype(BF16)


def project(first, attended, weight, done, whole, tile):
    tokens, width = attended.shape
    columns = weight.shape[1]
    more = [] if done is None else [done]
    return pl.pallas_call(
        project_kernel,
        out_shape=jax.ShapeDtypeStruct((tokens, whole), BF16),
        grid_spec=pltpu.PrefetchScalarGridSpec(
            num_scalar_prefetch=1,
            grid=(columns // tile,),
            in_specs=[
                pl.BlockSpec((tokens, width), lambda t, first: (0, 0)),
                pl.BlockSpec((width, tile), lambda t, first: (0, t)),
            ]
            + [pl.BlockSpec(memory_space=pl.ANY)] * len(more),
            out_specs=pl.BlockSpec((tokens, tile), lambda t, first: (0, first[0] + t)),
        ),
        input_output_aliases={} if done is None else {3: 0},
        compiler_params=pltpu.CompilerParams(vmem_limit_bytes=ROOM),
        cost_estimate=pl.CostEstimate(
            flops=2 * tokens * width * columns,
            bytes_accessed=2 * (width * columns + tokens * (width + columns)),
            transcendentals=0,
        ),
        name="project",
    )(first.astype(jnp.int32).reshape(1), attended, weight, *more)


def local(queries, cur_keys, cur_values, past_keys, past_values, pattern, read_blocks, out_weight):
    n = lax.axis_size("loop")
    groups = lax.axis_size("groups")
    me = lax.axis_index("loop")
    side = lax.axis_index("groups") % 2
    past_count, block_len, width = past_keys.shape
    length = queries.shape[0] // pattern.shape[0]
    list_len = read_blocks.shape[1]
    whole = out_weight.shape[1]
    piece = whole // 5
    tile = piece // 2
    mine = lax.all_gather(
        lax.dynamic_slice_in_dim(out_weight, side * piece, piece, 1), "loop", axis=0, tiled=True
    )
    rest = out_weight[:, 2 * piece :]
    bias_own, bias_other, wanted, place = plan(pattern, read_blocks, past_count, length, n, me)
    send = pick_blocks(wanted, past_keys, past_values, n, wanted.shape[0] // n)
    acc, mx, tot, got, part = near(
        queries, cur_keys, cur_values,
        past_keys.reshape(past_count * block_len, width),
        past_values.reshape(past_count * block_len, width),
        bias_own, send, n,
    )
    mine, rest, got = lax.optimization_barrier((mine, rest, got))
    rest = lax.all_gather(rest, "loop", axis=0, tiled=True)
    its = lax.ppermute(mine, "groups", [(i, i ^ 1) for i in range(groups)])
    attended = far(place, queries, part, got, bias_other, acc, mx, tot, list_len)
    done = project(2 * side, attended, mine, None, whole, tile)
    done = project(2 - 2 * side, attended, its, done, whole, tile)
    return project(jnp.full((), 4), attended, rest, done, whole, tile)


def solution(mesh):
    return jax.shard_map(
        local,
        mesh=mesh,
        in_specs=(
            P(("groups", "loop"), None),
            P(("groups", "loop"), None),
            P(("groups", "loop"), None),
            P(("groups", "loop"), None, None),
            P(("groups", "loop"), None, None),
            P(("groups", "loop"), None),
            P("groups", None),
            P("loop", None),
        ),
        out_specs=P(("groups", "loop"), None),
        check_vma=False,
    )
```
